256 devices in a mesh: pool: 2 (over core), ep: 128 (over x, z, y).
Axes of the slice: x: 4, y: 4, z: 8, core: 2. Of those that a mesh axis runs over, the one named last changes fastest.
Arguments:
- queries: bfloat16 [1024, 147456], P(('pool', 'ep')), may hold values from -90 to 90
- new_latent: bfloat16 [1024, 1152], P(('pool', 'ep')), may hold values from -6 to 6
- resident_cache: bfloat16 [768, 294912], P(('pool', 'ep')), may hold values from -6 to 6
- resident_len: int32 [768], P(('pool', 'ep')), may hold values from 1 to 512, as said below
- fresh_cache: bfloat16 [256, 294912], P(('pool', 'ep')), may hold values from -6 to 6
- fresh_len: int32 [2, 128], replicated, may hold values from 1 to 512, as said below
- matching: int32 [2, 128], replicated, may hold values from 0 to 127, each once within a row
Outputs:
- context: bfloat16 [1024, 131072], P(('pool', 'ep'))
The draws below stay inside these ranges and needn't reach their ends.
Inputs may be any that keep to these rules, and one draw needn't show every extreme that they name: `matching`: each row is a permutation. `resident_len`: some request has 512 positions. `fresh_len`: some request has 512 positions.
All inputs are finite; a program needn't handle non-finite values.
Results may differ from the reference program's by a relative error of at most 0.0048.
Values may be sent and summed in bfloat16 or wider, within the bound.
No kernel may reach another device: no remote copies, remote signals or barrier semaphores. Data moves between devices by JAX's collectives and lax.ppermute only.
A program may use at most 64 MiB of HBM per device.

```python
import jax
import jax.numpy as jnp
from jax import lax

HEADS = 128
LAT = 512
KV = 576
STEPS = 2
RES_DEV = 3
CTX = 512
ROWS = 4
TOKENS = 1024
RESIDENT = 768
N_POOL = 2
N_EP = 128
DEVICES = 256


def leading_cells(key):
    return jnp.clip(jax.random.normal(key, (RESIDENT, 2 * KV), jnp.float32), -6.0, 6.0)


def draw_resident_cache(key, part):
    leading = leading_cells(key)
    key = jax.random.fold_in(key, 5)
    remaining = jnp.clip(jax.random.normal(key, (RESIDENT, (CTX - 2) * KV), jnp.float32), -6.0, 6.0)
    return jnp.concatenate([leading, remaining], axis=1).astype(jnp.bfloat16)


def draw_queries(key, part):
    key = jax.random.fold_in(key, 7)
    values = jnp.clip(jax.random.normal(key, (TOKENS, STEPS * HEADS * KV), jnp.float32), -6.0, 6.0)
    return values.astype(jnp.bfloat16)


def draw_resident_len(key, part):
    key = jax.random.fold_in(key, 11)
    lengths = jax.random.randint(key, (RESIDENT,), 1, CTX + 1)
    chosen_spot = jax.random.randint(jax.random.fold_in(key, 1), (), 0, RESIDENT)
    return jnp.where(jnp.arange(RESIDENT) == chosen_spot, CTX, lengths).astype(jnp.int32)


def draw_fresh_len(key, part):
    key = jax.random.fold_in(key, 12)
    lengths = jax.random.randint(key, (N_POOL * N_EP,), 1, CTX + 1)
    chosen_spot = jax.random.randint(jax.random.fold_in(key, 1), (), 0, N_POOL * N_EP)
    lengths = jnp.where(jnp.arange(N_POOL * N_EP) == chosen_spot, CTX, lengths)
    return lengths.reshape(N_POOL, N_EP).astype(jnp.int32)


def levels(stream_key, shape, pieces, smallest, largest):
    def one(dim, blocks):
        steps = jax.random.uniform(jax.random.fold_in(jax.random.fold_in(stream_key, 6), dim), (blocks,), jnp.float32, smallest / len(pieces), largest / len(pieces))
        return jnp.repeat(jnp.exp(steps), shape[dim] // blocks).reshape((-1,) + (1,) * (len(shape) - dim - 1))

    loudness = one(*pieces[0])
    for cut in pieces[1:]:
        loudness = loudness * one(*cut)
    return loudness


def scatter_about(key, extent, spread, most, pieces=(), kind=jnp.bfloat16):
    loudness = levels(key, extent, pieces, -0.22, 0.18) if pieces else 1.0
    array = jax.random.normal(key, extent, jnp.float32) * spread * loudness
    return jnp.minimum(jnp.maximum(array, -most), most).astype(kind)


def setup_inputs(seed: int = 0) -> dict:
    splits = jax.random.split(jax.random.key(seed), 8)
    queries = draw_queries(jax.random.fold_in(splits[7], 71), 0)
    new_latent = scatter_about(splits[1], (TOKENS, STEPS * KV), 1.0, 6.0, ((0, 256),))
    resident_cache = draw_resident_cache(jax.random.fold_in(splits[7], 71), 0)
    resident_len = draw_resident_len(jax.random.fold_in(splits[7], 71), 0)
    fresh_cache = scatter_about(splits[4], (DEVICES, CTX * KV), 1.0, 6.0, ((0, 256),))
    fresh_len = draw_fresh_len(jax.random.fold_in(splits[7], 71), 0)
    matching = jax.vmap(lambda own: jax.random.permutation(own, N_EP))(jax.random.split(splits[6], N_POOL)).reshape((N_POOL, N_EP)).astype(jnp.int32)
    return dict(queries=queries, new_latent=new_latent, resident_cache=resident_cache, resident_len=resident_len, fresh_cache=fresh_cache, fresh_len=fresh_len, matching=matching)


score_scale = 192.0 ** -0.5


def attend(queries, caches, lengths, latents):
    q_full = queries.astype(jnp.float32)
    c_full = caches.astype(jnp.float32)
    n_full = latents.astype(jnp.float32)
    old_scores = jnp.einsum("rthk,rck->rthc", q_full, c_full) * score_scale
    new_scores = jnp.einsum("rthk,rsk->rths", q_full, n_full) * score_scale
    positions = jnp.arange(caches.shape[1], dtype=jnp.int32)
    live_old = (positions[None, :] < lengths[:, None])[:, None, None, :]
    step_order = jnp.arange(queries.shape[1], dtype=jnp.int32)
    live_new = (step_order[None, :] <= step_order[:, None])[None, :, None, :]
    old_scores = jnp.where(live_old, old_scores, -jnp.inf)
    new_scores = jnp.where(live_new, new_scores, -jnp.inf)
    peak_score = jnp.maximum(jnp.max(old_scores, axis=3, keepdims=True), jnp.max(new_scores, axis=3, keepdims=True))
    old_exp = jnp.exp(old_scores - peak_score)
    new_exp = jnp.exp(new_scores - peak_score)
    denominator = jnp.sum(old_exp, axis=3, keepdims=True) + jnp.sum(new_exp, axis=3, keepdims=True)
    old_probs = (old_exp / denominator).astype(jnp.bfloat16)
    new_probs = (new_exp / denominator).astype(jnp.bfloat16)
    context = jnp.einsum("rthc,rcl->rthl", old_probs.astype(jnp.float32), c_full[:, :, :LAT])
    context = context + jnp.einsum("rths,rsl->rthl", new_probs.astype(jnp.float32), n_full[:, :, :LAT])
    return context.astype(jnp.bfloat16)


def reference(queries, new_latent, resident_cache, resident_len, fresh_cache, fresh_len, matching):
    def one_device(device_index):
        pool_index = device_index // N_EP
        ep_index = device_index % N_EP
        partner = 1 - pool_index
        source = matching[pool_index, ep_index]
        arrived = lax.dynamic_slice_in_dim(fresh_cache, (partner * N_EP + source).astype(jnp.int32), 1, 0)
        arrive_len = fresh_len[partner, source]
        resident = lax.dynamic_slice_in_dim(resident_cache, (device_index * RES_DEV).astype(jnp.int32), RES_DEV, 0)
        own_lengths = lax.dynamic_slice_in_dim(resident_len, (device_index * RES_DEV).astype(jnp.int32), RES_DEV, 0)
        caches = jnp.concatenate([resident, arrived], axis=0).reshape(ROWS, CTX, KV)
        lengths = jnp.concatenate([own_lengths, arrive_len[None]]).astype(jnp.int32)
        block_queries = lax.dynamic_slice_in_dim(queries, (device_index * ROWS).astype(jnp.int32), ROWS, 0).reshape(ROWS, STEPS, HEADS, KV)
        block_latents = lax.dynamic_slice_in_dim(new_latent, (device_index * ROWS).astype(jnp.int32), ROWS, 0).reshape(ROWS, STEPS, KV)
        return attend(block_queries, caches, lengths, block_latents).reshape(ROWS, STEPS * HEADS * LAT)

    context = lax.map(one_device, jnp.arange(DEVICES, dtype=jnp.int32)).reshape(TOKENS, STEPS * HEADS * LAT)
    return context
```

```python
import jax
import jax.numpy as jnp
from jax import lax
from jax.experimental import pallas as pl
from jax.experimental.pallas import tpu as pltpu
from jax.sharding import PartitionSpec as P

LAT = 512
KV = 576
STEPS = 2
HEADS = 128
CTX = 512
LANES = 128
PAIRS = CTX // 2
PAIR_ROWS = 2 * KV // LANES
CACHE_ROWS = CTX * KV // LANES
QUERY_ROWS = STEPS * HEADS * KV // LANES
BF, F32 = jnp.bfloat16, jnp.float32

score_scale = 192.0 ** (-0.5)
in_vmem = pl.BlockSpec(memory_space=pltpu.VMEM)
in_smem = pl.BlockSpec(memory_space=pltpu.SMEM)
params = pltpu.CompilerParams(vmem_limit_bytes=40 << 20)


def flat_row(src, row, flat, count):
    for at in range(0, count, LANES):
        piece = src[pl.ds(row, 1), pl.ds(at * LANES, LANES * LANES)]
        flat[pl.ds(at, LANES), :] = piece.astype(F32).reshape(LANES, LANES)


def halves(tiles):
    even = jnp.concatenate(tiles[:5], axis=1)[:, :KV]
    odd = jnp.concatenate(tiles[4:], axis=1)[:, KV - LAT : KV - LAT + KV]
    return even, odd


def strided_halves(flat, pairs):
    return halves([flat[pl.ds(j, pairs, PAIR_ROWS), :].astype(BF) for j in range(PAIR_ROWS)])


def padded_latents(new, row):
    lat = new[pl.ds(row, 1), :].astype(F32)
    rows = [lat[:, s * KV : (s + 1) * KV] for s in range(STEPS)]
    return jnp.concatenate(rows + [jnp.zeros((8 - STEPS, KV), F32)], axis=0).astype(BF)


def attend(queries, key_even, key_odd, length, latents):
    both_last = (((1,), (1,)), ((), ()))

    def scores(keys):
        return lax.dot_general(queries, keys, both_last, preferred_element_type=F32) * score_scale

    even, odd, new = scores(key_even), scores(key_odd), scores(latents)
    position = 2 * lax.broadcasted_iota(jnp.int32, even.shape, 1)
    even = jnp.where(position < length, even, -jnp.inf)
    odd = jnp.where(position + 1 < length, odd, -jnp.inf)
    row = lax.broadcasted_iota(jnp.int32, new.shape, 0)
    step = jnp.where((row & (HEADS - 1)) >= HEADS // 2, 1, 0)
    new = jnp.where(lax.broadcasted_iota(jnp.int32, new.shape, 1) <= step, new, -jnp.inf)
    parts = (even, odd, new)
    peak = jnp.max(even, axis=1, keepdims=True)
    for part in parts[1:]:
        peak = jnp.maximum(peak, jnp.max(part, axis=1, keepdims=True))
    exps = [jnp.exp(part - peak) for part in parts]
    inverse = 1.0 / sum(jnp.sum(e, axis=1, keepdims=True) for e in exps)
    context = 0.0
    for e, values in zip(exps, (key_even, key_odd, latents)):
        probs = (e * inverse).astype(BF)
        context = context + jnp.dot(probs, values[:, :LAT], preferred_element_type=F32)
    return context.astype(BF)


def fresh_kernel(src, out, flat):
    flat_row(src, 0, flat, CACHE_ROWS)
    for g in range(PAIRS // 16):
        for j in range(PAIR_ROWS):
            tile = flat[pl.ds(g * 16 * PAIR_ROWS + j, 16, PAIR_ROWS), :]
            out[pl.ds((g * PAIR_ROWS + j) * 16, 16), :] = tile.astype(BF)


def fresh_tiles(fresh):
    return pl.pallas_call(
        fresh_kernel,
        out_shape=jax.ShapeDtypeStruct((CACHE_ROWS, LANES), BF),
        in_specs=[in_vmem],
        out_specs=in_vmem,
        scratch_shapes=[pltpu.VMEM((CACHE_ROWS, LANES), F32)],
        compiler_params=params,
        name="fresh_tiles",
    )(fresh)


def gather_kernel(sources, blocks, out):
    def some(i, carry):
        for u in range(8):
            out[i * 8 + u] = blocks[sources[i * 8 + u]]
        return carry

    lax.fori_loop(0, out.shape[0] // 8, some, 0)


def gather_blocks(sources, blocks):
    return pl.pallas_call(
        gather_kernel,
        out_shape=jax.ShapeDtypeStruct(blocks.shape, BF),
        in_specs=[in_smem, in_vmem],
        out_specs=in_vmem,
        compiler_params=params,
        name="gather_blocks",
    )(sources, blocks)


def resident_kernel(lengths, queries, new, caches, context, last_queries, last_latents, query_flat, cache_flat):
    def queries_of(row):
        flat_row(queries, row, query_flat, QUERY_ROWS)
        return jnp.concatenate(strided_halves(query_flat, QUERY_ROWS // PAIR_ROWS), axis=0)

    count = caches.shape[0]
    for r in range(count):
        flat_row(caches, r, cache_flat, CACHE_ROWS)
        key_even, key_odd = strided_halves(cache_flat, PAIRS)
        context[r] = attend(queries_of(r), key_even, key_odd, lengths[r], padded_latents(new, r))
    last_queries[...] = queries_of(count)
    last_latents[...] = padded_latents(new, count)


def resident_attention(lengths, queries, new, caches):
    count = caches.shape[0]
    return pl.pallas_call(
        resident_kernel,
        out_shape=(
            jax.ShapeDtypeStruct((count, STEPS * HEADS, LAT), BF),
            jax.ShapeDtypeStruct((STEPS * HEADS, KV), BF),
            jax.ShapeDtypeStruct((8, KV), BF),
        ),
        in_specs=[in_smem, in_vmem, in_vmem, in_vmem],
        out_specs=(in_vmem, in_vmem, in_vmem),
        scratch_shapes=[pltpu.VMEM((QUERY_ROWS, LANES), F32), pltpu.VMEM((CACHE_ROWS, LANES), F32)],
        compiler_params=params,
        cost_estimate=pl.CostEstimate(flops=10**9, bytes_accessed=8 << 20, transcendentals=400000),
        name="resident_attention",
    )(lengths, queries, new, caches)


def arrived_kernel(length, queries, latents, keys, resident, out):
    tiles = keys[...].reshape(PAIRS // 16, PAIR_ROWS, 16, LANES)
    key_even, key_odd = halves([tiles[:, j].reshape(PAIRS, LANES) for j in range(PAIR_ROWS)])
    count = resident.shape[0]
    out[0:count] = resident[...]
    out[count] = attend(queries[...], key_even, key_odd, length[0], latents[...])


def arrived_attention(length, queries, latents, keys, resident):
    return pl.pallas_call(
        arrived_kernel,
        out_shape=jax.ShapeDtypeStruct((resident.shape[0] + 1,) + resident.shape[1:], BF),
        in_specs=[in_smem, in_vmem, in_vmem, in_vmem, in_vmem],
        out_specs=in_vmem,
        compiler_params=params,
        name="arrived_attention",
    )(length, queries, latents, keys, resident)


def per_device(queries, new_latent, resident_cache, resident_len, fresh_cache, fresh_len, matching):
    group_count = lax.axis_size("ep")
    pool_index = lax.axis_index("pool")
    own_sources = matching[pool_index]
    tiles = fresh_tiles(fresh_cache)
    tiles = lax.ppermute(tiles, "pool", [(0, 1), (1, 0)])
    blocks = tiles.reshape(group_count, PAIR_ROWS, 2, LANES)
    blocks = lax.all_to_all(blocks, "ep", split_axis=0, concat_axis=0, tiled=True)
    resident, last_queries, last_latents = resident_attention(resident_len, queries, new_latent, resident_cache)
    blocks, resident = lax.optimization_barrier((blocks, resident))
    blocks = gather_blocks(own_sources, blocks)
    blocks = lax.all_to_all(blocks, "ep", split_axis=0, concat_axis=0, tiled=True)
    arrive_len = fresh_len[1 - pool_index, own_sources[lax.axis_index("ep")]]
    context = arrived_attention(
        arrive_len[None], last_queries, last_latents, blocks.reshape(CACHE_ROWS, LANES), resident
    )
    rows = context.shape[0]
    context = context.reshape(rows, 2, STEPS * HEADS // 2, LAT).transpose(0, 2, 1, 3)
    return context.reshape(rows, -1)


def solution(mesh):
    return jax.shard_map(
        per_device,
        mesh=mesh,
        in_specs=(
            P(("pool", "ep"), None),
            P(("pool", "ep"), None),
            P(("pool", "ep"), None),
            P(("pool", "ep")),
            P(("pool", "ep"), None),
            P(),
            P(),
        ),
        out_specs=P(("pool", "ep"), None),
        check_vma=False,
    )
```

```python
import jax
import jax.numpy as jnp
from jax import lax
from jax.experimental import pallas as pl
from jax.experimental.pallas import tpu as pltpu
from jax.sharding import PartitionSpec as P

LAT = 512
KV = 576
STEPS = 2
HEADS = 128
CTX = 512
ROWS = 4
LANES = 128
PAIRS = CTX // 2
PAIR_ROWS = 2 * KV // LANES
CACHE_ROWS = CTX * KV // LANES
QUERY_ROWS = STEPS * HEADS * KV // LANES
CHUNKS = STEPS * HEADS * LAT // LANES
GATHER_PIECES = 4
BF, F32 = jnp.bfloat16, jnp.float32

score_scale = 192.0 ** (-0.5)
in_vmem = pl.BlockSpec(memory_space=pltpu.VMEM)
in_smem = pl.BlockSpec(memory_space=pltpu.SMEM)
small = pltpu.CompilerParams(vmem_limit_bytes=8 << 20)


def flat_row(src, row, flat, count):
    for at in range(0, count, LANES):
        piece = src[pl.ds(row, 1), pl.ds(at * LANES, LANES * LANES)]
        flat[pl.ds(at, LANES), :] = piece.astype(F32).reshape(LANES, LANES)


def halves(tiles):
    even = jnp.concatenate(tiles[:5], axis=1)[:, :KV]
    odd = jnp.concatenate(tiles[4:], axis=1)[:, KV - LAT : KV - LAT + KV]
    return even, odd


def strided_halves(flat, pairs):
    return halves([flat[pl.ds(j, pairs, PAIR_ROWS), :].astype(BF) for j in range(PAIR_ROWS)])


def padded_latents(new, row):
    lat = new[pl.ds(row, 1), :].astype(F32)
    rows = [lat[:, s * KV : (s + 1) * KV] for s in range(STEPS)]
    return jnp.concatenate(rows + [jnp.zeros((LANES - STEPS, KV), F32)], axis=0).astype(BF)


def by_step(even, odd):
    half = HEADS // 2
    return jnp.concatenate([x[s * half : (s + 1) * half] for s in range(STEPS) for x in (even, odd)], axis=0)


def probabilities(queries, keys, length):
    scores = lax.dot_general(queries, keys, (((1,), (1,)), ((), ())), preferred_element_type=F32) * score_scale
    column = lax.broadcasted_iota(jnp.int32, (1, CTX + LANES), 1)
    position = jnp.where(column < PAIRS, 2 * column, 2 * (column - PAIRS) + 1)
    step = lax.broadcasted_iota(jnp.int32, (STEPS * HEADS, 1), 0) >> (HEADS - 1).bit_length()
    live = jnp.where(column < CTX, position, column - CTX) < jnp.where(column < CTX, length, step + 1)
    scores = jnp.where(live, scores, -jnp.inf)
    exps = jnp.exp(scores - jnp.max(scores, axis=1, keepdims=True))
    return (exps * (1.0 / jnp.sum(exps, axis=1, keepdims=True))).astype(BF)


def put_context(rows, token, step, context):
    tokens = rows.shape[0] // CHUNKS
    half, chunks = HEADS // 2, LAT // LANES
    for parity in range(2):
        for k in range(chunks):
            at = (step * HEADS * chunks + parity * chunks + k) * tokens + token % tokens
            rows[pl.ds(at, half, 2 * chunks * tokens), :] = context[
                parity * half : (parity + 1) * half, k * LANES : (k + 1) * LANES
            ]


def fresh_kernel(src, out, flat):
    flat_row(src, 0, flat, CACHE_ROWS)
    for g in range(PAIRS // 16):
        for j in range(PAIR_ROWS):
            tile = flat[pl.ds(g * 16 * PAIR_ROWS + j, 16, PAIR_ROWS), :]
            out[pl.ds((g * PAIR_ROWS + j) * 16, 16), :] = tile.astype(BF)


def fresh_tiles(fresh):
    return pl.pallas_call(
        fresh_kernel,
        out_shape=jax.ShapeDtypeStruct((CACHE_ROWS, LANES), BF),
        in_specs=[in_vmem],
        out_specs=in_vmem,
        scratch_shapes=[pltpu.VMEM((CACHE_ROWS, LANES), F32)],
        compiler_params=small,
        name="fresh_tiles",
    )(fresh)


def gather_kernel(sources, blocks, out, picked, sems):
    size = out.shape[0] // GATHER_PIECES
    copies = []
    for piece in range(GATHER_PIECES):
        at = piece * size
        for d in range(at, at + size):
            picked[d] = blocks[sources[d]]
        copy = pltpu.make_async_copy(picked.at[pl.ds(at, size)], out.at[pl.ds(at, size)], sems.at[piece])
        copy.start()
        copies.append(copy)
    for copy in copies:
        copy.wait()


def gather_blocks(sources, blocks):
    return pl.pallas_call(
        gather_kernel,
        out_shape=jax.ShapeDtypeStruct(blocks.shape, BF),
        in_specs=[in_smem, in_vmem],
        out_specs=pl.BlockSpec(memory_space=pl.ANY),
        scratch_shapes=[pltpu.VMEM(blocks.shape, BF), pltpu.SemaphoreType.DMA((GATHER_PIECES,))],
        compiler_params=small,
        name="gather_blocks",
    )(sources, blocks)


def resident_kernel(
    lengths, queries, new, caches, out, third, last_queries, last_latents, query_flat, cache_flat, rows
):
    def queries_of(row):
        flat_row(queries, row, query_flat, QUERY_ROWS)
        return by_step(*strided_halves(query_flat, QUERY_ROWS // PAIR_ROWS))

    for r in range(ROWS - 1):
        flat_row(caches, r, cache_flat, CACHE_ROWS)
        keys = jnp.concatenate([*strided_halves(cache_flat, PAIRS), padded_latents(new, r)], axis=0)
        probs = probabilities(queries_of(r), keys, lengths[r])
        context = jnp.dot(probs, keys[:, :LAT], preferred_element_type=F32)
        for step in range(STEPS):
            put_context(rows, r, step, context[step * HEADS : (step + 1) * HEADS])
    for c in range(0, CHUNKS, LANES):
        piece = rows[pl.ds(c * ROWS, LANES * ROWS), :]
        out[pl.ds(c, LANES)] = piece.astype(BF).reshape(LANES, 2, 2, LANES)
    third[...] = rows[pl.ds(ROWS - 2, CHUNKS, ROWS), :]
    last_queries[...] = queries_of(ROWS - 1)
    last_latents[...] = padded_latents(new, ROWS - 1)


def resident_attention(lengths, queries, new, caches):
    return pl.pallas_call(
        resident_kernel,
        out_shape=(
            jax.ShapeDtypeStruct((CHUNKS, 2, 2, LANES), BF),
            jax.ShapeDtypeStruct((CHUNKS, LANES), F32),
            jax.ShapeDtypeStruct((STEPS * HEADS, KV), BF),
            jax.ShapeDtypeStruct((LANES, KV), BF),
        ),
        in_specs=[in_smem, in_vmem, in_vmem, in_vmem],
        out_specs=(in_vmem,) * 4,
        scratch_shapes=[
            pltpu.VMEM((QUERY_ROWS, LANES), F32),
            pltpu.VMEM((CACHE_ROWS, LANES), F32),
            pltpu.VMEM((ROWS * CHUNKS, LANES), F32),
        ],
        compiler_params=pltpu.CompilerParams(vmem_limit_bytes=32 << 20),
        cost_estimate=pl.CostEstimate(flops=10**9, bytes_accessed=8 << 20, transcendentals=400000),
        name="resident_attention",
    )(lengths, queries, new, caches)


def arrived_kernel(length, queries, latents, tiles, third, before, out, both, rows, sems):
    parts = tiles[...].reshape(PAIRS // 16, PAIR_ROWS, 16, LANES)
    halved = halves([parts[:, j].reshape(PAIRS, LANES) for j in range(PAIR_ROWS)])
    keys = jnp.concatenate([*halved, latents[...]], axis=0)
    both[pl.ds(0, CHUNKS, 2), :] = third[...]
    probs = probabilities(queries[...], keys, length[0])
    values = keys[:, :LAT]
    copies = []
    size = CHUNKS // STEPS
    for step in range(STEPS):
        context = jnp.dot(probs[step * HEADS : (step + 1) * HEADS], values, preferred_element_type=F32)
        put_context(both, ROWS - 1, step, context)
        place = pl.ds(step * size, size)
        for c in range(step * size, (step + 1) * size, LANES):
            rows[pl.ds(c, LANES)] = both[pl.ds(2 * c, 2 * LANES), :].astype(BF).reshape(LANES, 2, LANES)
        copy = pltpu.make_async_copy(rows.at[place], out.at[place, 1], sems.at[step])
        copy.start()
        copies.append(copy)
    for copy in copies:
        copy.wait()


def arrived_attention(length, queries, latents, tiles, third, before):
    whole = pl.BlockSpec(memory_space=pl.ANY)
    return pl.pallas_call(
        arrived_kernel,
        out_shape=jax.ShapeDtypeStruct(before.shape, BF),
        in_specs=[in_smem, in_vmem, in_vmem, in_vmem, in_vmem, whole],
        out_specs=whole,
        scratch_shapes=[
            pltpu.VMEM((2 * CHUNKS, LANES), F32),
            pltpu.VMEM((CHUNKS, 2, LANES), BF),
            pltpu.SemaphoreType.DMA((STEPS,)),
        ],
        input_output_aliases={5: 0},
        compiler_params=pltpu.CompilerParams(vmem_limit_bytes=24 << 20),
        name="arrived_attention",
    )(length, queries, latents, tiles, third, before)


def per_device(queries, new_latent, resident_cache, resident_len, fresh_cache, fresh_len, matching):
    group_count = lax.axis_size("ep")
    pool_index = lax.axis_index("pool")
    own_sources = matching[pool_index]
    tiles = fresh_tiles(fresh_cache)
    tiles = lax.ppermute(tiles, "pool", [(0, 1), (1, 0)])
    blocks = tiles.reshape(group_count, PAIR_ROWS, 2, LANES)
    blocks = lax.all_to_all(blocks, "ep", split_axis=0, concat_axis=0, tiled=True)
    out, third, last_queries, last_latents = resident_attention(resident_len, queries, new_latent, resident_cache)
    blocks, third = lax.optimization_barrier((blocks, third))
    blocks = gather_blocks(own_sources, blocks)
    blocks = lax.all_to_all(blocks, "ep", split_axis=0, concat_axis=0, tiled=True)
    arrive_len = fresh_len[1 - pool_index, own_sources[lax.axis_index("ep")]]
    tiles = blocks.reshape(CACHE_ROWS, LANES)
    out = arrived_attention(arrive_len[None], last_queries, last_latents, tiles, third, out)
    return out.transpose(1, 2, 0, 3).reshape(ROWS, -1)


def solution(mesh):
    return jax.shard_map(
        per_device,
        mesh=mesh,
        in_specs=(
            P(("pool", "ep"), None),
            P(("pool", "ep"), None),
            P(("pool", "ep"), None),
            P(("pool", "ep")),
            P(("pool", "ep"), None),
            P(),
            P(),
        ),
        out_specs=P(("pool", "ep"), None),
        check_vma=False,
    )
```

```python
import jax
import jax.numpy as jnp
from jax import lax
from jax.experimental import pallas as pl
from jax.experimental.pallas import tpu as pltpu
from jax.sharding import PartitionSpec as P

LAT = 512
KV = 576
STEPS = 2
HEADS = 128
CTX = 512
ROWS = 4
LANES = 128
PAIRS = CTX // 2
PAIR_ROWS = 2 * KV // LANES
CACHE_ROWS = CTX * KV // LANES
QUERY_ROWS = STEPS * HEADS * KV // LANES
CHUNKS = STEPS * HEADS * LAT // LANES
BF, F32 = jnp.bfloat16, jnp.float32

score_scale = 192.0 ** (-0.5)
in_vmem = pl.BlockSpec(memory_space=pltpu.VMEM)
in_smem = pl.BlockSpec(memory_space=pltpu.SMEM)
small = pltpu.CompilerParams(vmem_limit_bytes=8 << 20)


def flat_row(src, row, flat, count):
    for at in range(0, count, LANES):
        piece = src[pl.ds(row, 1), pl.ds(at * LANES, LANES * LANES)]
        flat[pl.ds(at, LANES), :] = piece.astype(F32).reshape(LANES, LANES)


def halves(tiles):
    even = jnp.concatenate(tiles[:5], axis=1)[:, :KV]
    odd = jnp.concatenate(tiles[4:], axis=1)[:, KV - LAT : KV - LAT + KV]
    return even, odd


def strided_halves(flat, pairs):
    return halves([flat[pl.ds(j, pairs, PAIR_ROWS), :].astype(BF) for j in range(PAIR_ROWS)])


def padded_latents(new, row):
    lat = new[pl.ds(row, 1), :].astype(F32)
    rows = [lat[:, s * KV : (s + 1) * KV] for s in range(STEPS)]
    return jnp.concatenate(rows + [jnp.zeros((LANES - STEPS, KV), F32)], axis=0).astype(BF)


def by_step(even, odd):
    half = HEADS // 2
    return jnp.concatenate([x[s * half : (s + 1) * half] for s in range(STEPS) for x in (even, odd)], axis=0)


def penalty(length):
    column = lax.broadcasted_iota(jnp.int32, (8, CTX + LANES), 1)
    position = jnp.where(column < PAIRS, 2 * column, 2 * (column - PAIRS) + 1)
    step = lax.broadcasted_iota(jnp.int32, (8, CTX + LANES), 0)
    live = jnp.where(column < CTX, position, column - CTX) < jnp.where(column < CTX, length, step + 1)
    return jnp.where(live, 0.0, -jnp.inf).astype(F32)


def probabilities(queries, keys, penalties):
    scores = lax.dot_general(queries, keys, (((1,), (1,)), ((), ())), preferred_element_type=F32) * score_scale
    rows = [scores[s * HEADS : (s + 1) * HEADS] + penalties[s : s + 1] for s in range(STEPS)]
    scores = jnp.concatenate(rows, axis=0)
    exps = jnp.exp(scores - jnp.max(scores, axis=1, keepdims=True))
    return (exps * (1.0 / jnp.sum(exps, axis=1, keepdims=True))).astype(BF)


def put_context(rows, token, step, context):
    tokens = rows.shape[0] // CHUNKS
    half, chunks = HEADS // 2, LAT // LANES
    for parity in range(2):
        for k in range(chunks):
            at = (step * HEADS * chunks + parity * chunks + k) * tokens + token % tokens
            rows[pl.ds(at, half, 2 * chunks * tokens), :] = context[
                parity * half : (parity + 1) * half, k * LANES : (k + 1) * LANES
            ]


def fresh_kernel(src, out, flat):
    flat_row(src, 0, flat, CACHE_ROWS)
    for g in range(PAIRS // 16):
        for j in range(PAIR_ROWS):
            tile = flat[pl.ds(g * 16 * PAIR_ROWS + j, 16, PAIR_ROWS), :]
            out[pl.ds((g * PAIR_ROWS + j) * 16, 16), :] = tile.astype(BF)


def fresh_tiles(fresh):
    return pl.pallas_call(
        fresh_kernel,
        out_shape=jax.ShapeDtypeStruct((CACHE_ROWS, LANES), BF),
        in_specs=[in_vmem],
        out_specs=in_vmem,
        scratch_shapes=[pltpu.VMEM((CACHE_ROWS, LANES), F32)],
        compiler_params=small,
        name="fresh_tiles",
    )(fresh)


def gather_kernel(sources, blocks, out):
    for d in range(out.shape[0]):
        out[d] = blocks[sources[d]]


def gather_blocks(sources, blocks):
    return pl.pallas_call(
        gather_kernel,
        out_shape=jax.ShapeDtypeStruct(blocks.shape, BF),
        in_specs=[in_smem, in_vmem],
        out_specs=in_vmem,
        compiler_params=small,
        name="gather_blocks",
    )(sources, blocks)


def pair_rows(both, rows, place):
    for c in range(place.start, place.start + place.size, LANES):
        rows[pl.ds(c, LANES)] = both[pl.ds(2 * c, 2 * LANES), :].astype(BF).reshape(LANES, 2, LANES)


def resident_kernel(
    lengths,
    fresh_lengths,
    matching,
    queries,
    new,
    caches,
    out,
    third,
    last_queries,
    last_latents,
    last_penalty,
    query_flat,
    cache_flat,
    both,
    rows,
    sem,
):
    def queries_of(row):
        flat_row(queries, row, query_flat, QUERY_ROWS)
        return by_step(*strided_halves(query_flat, QUERY_ROWS // PAIR_ROWS))

    for r in range(ROWS - 1):
        flat_row(caches, r, cache_flat, CACHE_ROWS)
        keys = jnp.concatenate([*strided_halves(cache_flat, PAIRS), padded_latents(new, r)], axis=0)
        probs = probabilities(queries_of(r), keys, penalty(lengths[r]))
        context = jnp.dot(probs, keys[:, :LAT], preferred_element_type=F32)
        for step in range(STEPS):
            put_context(both if r < 2 else third, r, step, context[step * HEADS : (step + 1) * HEADS])
        if r == 1:
            pair_rows(both, rows, pl.ds(0, CHUNKS))
            copy = pltpu.make_async_copy(rows, out.at[:, 0], sem)
            copy.start()
    last_queries[...] = queries_of(ROWS - 1)
    last_latents[...] = padded_latents(new, ROWS - 1)
    pool = lax.axis_index("pool")
    last_penalty[...] = penalty(fresh_lengths[1 - pool, matching[pool, lax.axis_index("ep")]])
    copy.wait()


def resident_attention(lengths, fresh_lengths, matching, queries, new, caches):
    return pl.pallas_call(
        resident_kernel,
        out_shape=(
            jax.ShapeDtypeStruct((CHUNKS, 2, 2, LANES), BF),
            jax.ShapeDtypeStruct((CHUNKS, LANES), F32),
            jax.ShapeDtypeStruct((STEPS * HEADS, KV), BF),
            jax.ShapeDtypeStruct((LANES, KV), BF),
            jax.ShapeDtypeStruct((8, CTX + LANES), F32),
        ),
        in_specs=[in_smem] * 3 + [in_vmem] * 3,
        out_specs=(pl.BlockSpec(memory_space=pl.ANY),) + (in_vmem,) * 4,
        scratch_shapes=[
            pltpu.VMEM((QUERY_ROWS, LANES), F32),
            pltpu.VMEM((CACHE_ROWS, LANES), F32),
            pltpu.VMEM((2 * CHUNKS, LANES), F32),
            pltpu.VMEM((CHUNKS, 2, LANES), BF),
            pltpu.SemaphoreType.DMA(()),
        ],
        compiler_params=pltpu.CompilerParams(vmem_limit_bytes=32 << 20),
        cost_estimate=pl.CostEstimate(flops=10**9, bytes_accessed=8 << 20, transcendentals=400000),
        name="resident_attention",
    )(lengths, fresh_lengths, matching, queries, new, caches)


def arrived_kernel(penalties, queries, latents, tiles, third, before, out, both, rows, sems):
    parts = tiles[...].reshape(PAIRS // 16, PAIR_ROWS, 16, LANES)
    halved = halves([parts[:, j].reshape(PAIRS, LANES) for j in range(PAIR_ROWS)])
    keys = jnp.concatenate([*halved, latents[...]], axis=0)
    both[pl.ds(0, CHUNKS, 2), :] = third[...]
    probs = probabilities(queries[...], keys, penalties[...])
    values = keys[:, :LAT]
    copies = []
    size = CHUNKS // STEPS
    for step in range(STEPS):
        context = jnp.dot(probs[step * HEADS : (step + 1) * HEADS], values, preferred_element_type=F32)
        put_context(both, ROWS - 1, step, context)
        place = pl.ds(step * size, size)
        pair_rows(both, rows, place)
        copy = pltpu.make_async_copy(rows.at[place], out.at[place, 1], sems.at[step])
        copy.start()
        copies.append(copy)
    for copy in copies:
        copy.wait()


def arrived_attention(penalties, queries, latents, tiles, third, before):
    whole = pl.BlockSpec(memory_space=pl.ANY)
    return pl.pallas_call(
        arrived_kernel,
        out_shape=jax.ShapeDtypeStruct(before.shape, BF),
        in_specs=[in_vmem] * 5 + [whole],
        out_specs=whole,
        scratch_shapes=[
            pltpu.VMEM((2 * CHUNKS, LANES), F32),
            pltpu.VMEM((CHUNKS, 2, LANES), BF),
            pltpu.SemaphoreType.DMA((STEPS,)),
        ],
        input_output_aliases={5: 0},
        compiler_params=pltpu.CompilerParams(vmem_limit_bytes=24 << 20),
        name="arrived_attention",
    )(penalties, queries, latents, tiles, third, before)


def per_device(queries, new_latent, resident_cache, resident_len, fresh_cache, fresh_len, matching):
    group_count = lax.axis_size("ep")
    pool_index = lax.axis_index("pool")
    own_sources = matching[pool_index]
    tiles = fresh_tiles(fresh_cache)
    tiles = lax.ppermute(tiles, "pool", [(0, 1), (1, 0)])
    blocks = tiles.reshape(group_count, PAIR_ROWS, 2, LANES)
    blocks = lax.all_to_all(blocks, "ep", split_axis=0, concat_axis=0, tiled=True)
    out, third, last_queries, last_latents, penalties = resident_attention(
        resident_len, fresh_len, matching, queries, new_latent, resident_cache
    )
    blocks, third = lax.optimization_barrier((blocks, third))
    blocks = gather_blocks(own_sources, blocks)
    blocks = lax.all_to_all(blocks, "ep", split_axis=0, concat_axis=0, tiled=True)
    tiles = blocks.reshape(CACHE_ROWS, LANES)
    out = arrived_attention(penalties, last_queries, last_latents, tiles, third, out)
    return out.transpose(1, 2, 0, 3).reshape(ROWS, -1)


def solution(mesh):
    return jax.shard_map(
        per_device,
        mesh=mesh,
        in_specs=(
            P(("pool", "ep"), None),
            P(("pool", "ep"), None),
            P(("pool", "ep"), None),
            P(("pool", "ep")),
            P(("pool", "ep"), None),
            P(),
            P(),
        ),
        out_specs=P(("pool", "ep"), None),
        check_vma=False,
    )
```

```python
import jax
import jax.numpy as jnp
from jax import lax
from jax.experimental import pallas as pl
from jax.experimental.pallas import tpu as pltpu
from jax.sharding import PartitionSpec as P

LAT = 512
KV = 576
STEPS = 2
HEADS = 128
CTX = 512
ROWS = 4
LANES = 128
PAIRS = CTX // 2
PAIR_ROWS = 2 * KV // LANES
CACHE_ROWS = CTX * KV // LANES
QUERY_ROWS = STEPS * HEADS * KV // LANES
CHUNKS = STEPS * HEADS * LAT // LANES
BF, F32 = jnp.bfloat16, jnp.float32

score_scale = 192.0 ** (-0.5)
in_vmem = pl.BlockSpec(memory_space=pltpu.VMEM)
in_smem = pl.BlockSpec(memory_space=pltpu.SMEM)
small = pltpu.CompilerParams(vmem_limit_bytes=8 << 20)


def flat_row(src, row, flat, count):
    for at in range(0, count, LANES):
        piece = src[pl.ds(row, 1), pl.ds(at * LANES, LANES * LANES)]
        flat[pl.ds(at, LANES), :] = piece.astype(F32).reshape(LANES, LANES)


def halves(tiles):
    even = jnp.concatenate(tiles[:5], axis=1)[:, :KV]
    odd = jnp.concatenate(tiles[4:], axis=1)[:, KV - LAT : KV - LAT + KV]
    return even, odd


def strided_halves(flat, pairs):
    return halves([flat[pl.ds(j, pairs, PAIR_ROWS), :].astype(BF) for j in range(PAIR_ROWS)])


def padded_latents(new, row):
    lat = new[pl.ds(row, 1), :].astype(F32)
    rows = [lat[:, s * KV : (s + 1) * KV] for s in range(STEPS)]
    return jnp.concatenate(rows + [jnp.zeros((LANES - STEPS, KV), F32)], axis=0).astype(BF)


def by_step(even, odd):
    half = HEADS // 2
    return jnp.concatenate([x[s * half : (s + 1) * half] for s in range(STEPS) for x in (even, odd)], axis=0)


def penalty(length):
    column = lax.broadcasted_iota(jnp.int32, (8, CTX + LANES), 1)
    position = jnp.where(column < PAIRS, 2 * column, 2 * (column - PAIRS) + 1)
    step = lax.broadcasted_iota(jnp.int32, (8, CTX + LANES), 0)
    live = jnp.where(column < CTX, position, column - CTX) < jnp.where(column < CTX, length, step + 1)
    return jnp.where(live, 0.0, -jnp.inf).astype(F32)


def probabilities(queries, keys, penalties):
    scores = lax.dot_general(queries, keys, (((1,), (1,)), ((), ())), preferred_element_type=F32) * score_scale
    rows = [scores[s * HEADS : (s + 1) * HEADS] + penalties[s : s + 1] for s in range(STEPS)]
    scores = jnp.concatenate(rows, axis=0)
    exps = jnp.exp(scores - jnp.max(scores, axis=1, keepdims=True))
    return (exps * (1.0 / jnp.sum(exps, axis=1, keepdims=True))).astype(BF)


def put_context(rows, token, step, context):
    tokens = rows.shape[0] // CHUNKS
    half, chunks = HEADS // 2, LAT // LANES
    for parity in range(2):
        for k in range(chunks):
            at = (step * HEADS * chunks + parity * chunks + k) * tokens + token % tokens
            rows[pl.ds(at, half, 2 * chunks * tokens), :] = context[
                parity * half : (parity + 1) * half, k * LANES : (k + 1) * LANES
            ]


def fresh_kernel(src, out, flat):
    flat_row(src, 0, flat, CACHE_ROWS)
    for g in range(PAIRS // 16):
        for j in range(PAIR_ROWS):
            tile = flat[pl.ds(g * 16 * PAIR_ROWS + j, 16, PAIR_ROWS), :]
            out[pl.ds((g * PAIR_ROWS + j) * 16, 16), :] = tile.astype(BF)


def fresh_tiles(fresh):
    return pl.pallas_call(
        fresh_kernel,
        out_shape=jax.ShapeDtypeStruct((CACHE_ROWS, LANES), BF),
        in_specs=[in_vmem],
        out_specs=in_vmem,
        scratch_shapes=[pltpu.VMEM((CACHE_ROWS, LANES), F32)],
        compiler_params=small,
        name="fresh_tiles",
    )(fresh)


def gather_kernel(sources, blocks, out):
    last = out.shape[0] - 1
    for d in range(last + 1):
        out[d] = blocks[last - sources[last - d]]


def gather_blocks(sources, blocks):
    return pl.pallas_call(
        gather_kernel,
        out_shape=jax.ShapeDtypeStruct(blocks.shape, BF),
        in_specs=[in_smem, in_vmem],
        out_specs=in_vmem,
        compiler_params=small,
        name="gather_blocks",
    )(sources, blocks)


def pair_rows(both, rows, place):
    for c in range(place.start, place.start + place.size, LANES):
        rows[pl.ds(c, LANES)] = both[pl.ds(2 * c, 2 * LANES), :].astype(BF).reshape(LANES, 2, LANES)


def resident_kernel(
    lengths,
    fresh_lengths,
    matching,
    queries,
    new,
    caches,
    out,
    third,
    last_queries,
    last_latents,
    last_penalty,
    query_flat,
    cache_flat,
    both,
    rows,
    sem,
):
    def queries_of(row):
        flat_row(queries, row, query_flat, QUERY_ROWS)
        return by_step(*strided_halves(query_flat, QUERY_ROWS // PAIR_ROWS))

    for r in range(ROWS - 1):
        flat_row(caches, r, cache_flat, CACHE_ROWS)
        keys = jnp.concatenate([*strided_halves(cache_flat, PAIRS), padded_latents(new, r)], axis=0)
        probs = probabilities(queries_of(r), keys, penalty(lengths[r]))
        context = jnp.dot(probs, keys[:, :LAT], preferred_element_type=F32)
        for step in range(STEPS):
            put_context(both if r < 2 else third, r, step, context[step * HEADS : (step + 1) * HEADS])
        if r == 1:
            pair_rows(both, rows, pl.ds(0, CHUNKS))
            copy = pltpu.make_async_copy(rows, out.at[:, 0], sem)
            copy.start()
    last_queries[...] = queries_of(ROWS - 1)
    last_latents[...] = padded_latents(new, ROWS - 1)
    pool = lax.axis_index("pool")
    last_penalty[...] = penalty(fresh_lengths[1 - pool, matching[pool, lax.axis_index("ep")]])
    copy.wait()


def resident_attention(lengths, fresh_lengths, matching, queries, new, caches):
    return pl.pallas_call(
        resident_kernel,
        out_shape=(
            jax.ShapeDtypeStruct((CHUNKS, 2, 2, LANES), BF),
            jax.ShapeDtypeStruct((CHUNKS, LANES), F32),
            jax.ShapeDtypeStruct((STEPS * HEADS, KV), BF),
            jax.ShapeDtypeStruct((LANES, KV), BF),
            jax.ShapeDtypeStruct((8, CTX + LANES), F32),
        ),
        in_specs=[in_smem] * 3 + [in_vmem] * 3,
        out_specs=(pl.BlockSpec(memory_space=pl.ANY),) + (in_vmem,) * 4,
        scratch_shapes=[
            pltpu.VMEM((QUERY_ROWS, LANES), F32),
            pltpu.VMEM((CACHE_ROWS, LANES), F32),
            pltpu.VMEM((2 * CHUNKS, LANES), F32),
            pltpu.VMEM((CHUNKS, 2, LANES), BF),
            pltpu.SemaphoreType.DMA(()),
        ],
        compiler_params=pltpu.CompilerParams(vmem_limit_bytes=32 << 20),
        cost_estimate=pl.CostEstimate(flops=10**9, bytes_accessed=8 << 20, transcendentals=400000),
        name="resident_attention",
    )(lengths, fresh_lengths, matching, queries, new, caches)


def arrived_kernel(penalties, queries, latents, tiles, third, before, out, both, rows, sems):
    parts = tiles[...].reshape(PAIRS // 16, PAIR_ROWS, 16, LANES)
    halved = halves([parts[:, j].reshape(PAIRS, LANES) for j in range(PAIR_ROWS)])
    keys = jnp.concatenate([*halved, latents[...]], axis=0)
    both[pl.ds(0, CHUNKS, 2), :] = third[...]
    probs = probabilities(queries[...], keys, penalties[...])
    values = keys[:, :LAT]
    copies = []
    size = CHUNKS // STEPS
    for step in range(STEPS):
        context = jnp.dot(probs[step * HEADS : (step + 1) * HEADS], values, preferred_element_type=F32)
        put_context(both, ROWS - 1, step, context)
        place = pl.ds(step * size, size)
        pair_rows(both, rows, place)
        copy = pltpu.make_async_copy(rows.at[place], out.at[place, 1], sems.at[step])
        copy.start()
        copies.append(copy)
    for copy in copies:
        copy.wait()


def arrived_attention(penalties, queries, latents, tiles, third, before):
    whole = pl.BlockSpec(memory_space=pl.ANY)
    return pl.pallas_call(
        arrived_kernel,
        out_shape=jax.ShapeDtypeStruct(before.shape, BF),
        in_specs=[in_vmem] * 5 + [whole],
        out_specs=whole,
        scratch_shapes=[
            pltpu.VMEM((2 * CHUNKS, LANES), F32),
            pltpu.VMEM((CHUNKS, 2, LANES), BF),
            pltpu.SemaphoreType.DMA((STEPS,)),
        ],
        input_output_aliases={5: 0},
        compiler_params=pltpu.CompilerParams(vmem_limit_bytes=24 << 20),
        name="arrived_attention",
    )(penalties, queries, latents, tiles, third, before)


def exchange(blocks):
    places = list(range(blocks.shape[0]))[::-1]
    return lax.all_to_all(blocks, "ep", split_axis=0, concat_axis=0, tiled=True, axis_index_groups=[places])


def per_device(queries, new_latent, resident_cache, resident_len, fresh_cache, fresh_len, matching):
    group_count = lax.axis_size("ep")
    pool_index = lax.axis_index("pool")
    own_sources = matching[pool_index]
    tiles = fresh_tiles(fresh_cache)
    tiles = lax.ppermute(tiles, "pool", [(0, 1), (1, 0)])
    blocks = tiles.reshape(group_count, PAIR_ROWS, 2, LANES)
    blocks = exchange(blocks)
    out, third, last_queries, last_latents, penalties = resident_attention(
        resident_len, fresh_len, matching, queries, new_latent, resident_cache
    )
    blocks, third = lax.optimization_barrier((blocks, third))
    blocks = gather_blocks(own_sources, blocks)
    blocks = exchange(blocks)
    tiles = blocks.reshape(CACHE_ROWS, LANES)
    out = arrived_attention(penalties, last_queries, last_latents, tiles, third, out)
    return out.transpose(1, 2, 0, 3).reshape(ROWS, -1)


def solution(mesh):
    return jax.shard_map(
        per_device,
        mesh=mesh,
        in_specs=(
            P(("pool", "ep"), None),
            P(("pool", "ep"), None),
            P(("pool", "ep"), None),
            P(("pool", "ep")),
            P(("pool", "ep"), None),
            P(),
            P(),
        ),
        out_specs=P(("pool", "ep"), None),
        check_vma=False,
    )
```

```python
import jax
import jax.numpy as jnp
from jax import lax
from jax.experimental import pallas as pl
from jax.experimental.pallas import tpu as pltpu
from jax.sharding import PartitionSpec as P

LAT = 512
KV = 576
STEPS = 2
HEADS = 128
CTX = 512
ROWS = 4
LANES = 128
PAIRS = CTX // 2
PAIR_ROWS = 2 * KV // LANES
CACHE_ROWS = CTX * KV // LANES
QUERY_ROWS = STEPS * HEADS * KV // LANES
CHUNKS = STEPS * HEADS * LAT // LANES
BF, F32 = jnp.bfloat16, jnp.float32

score_scale = 192.0 ** (-0.5)
in_vmem = pl.BlockSpec(memory_space=pltpu.VMEM)
in_smem = pl.BlockSpec(memory_space=pltpu.SMEM)
small = pltpu.CompilerParams(vmem_limit_bytes=8 << 20)


def flat_row(src, row, flat, count):
    for at in range(0, count, LANES):
        piece = src[pl.ds(row, 1), pl.ds(at * LANES, LANES * LANES)]
        flat[pl.ds(at, LANES), :] = piece.astype(F32).reshape(LANES, LANES)


def halves(tiles):
    even = jnp.concatenate(tiles[:5], axis=1)[:, :KV]
    odd = jnp.concatenate(tiles[4:], axis=1)[:, KV - LAT : KV - LAT + KV]
    return even, odd


def strided_halves(flat, pairs):
    return halves([flat[pl.ds(j, pairs, PAIR_ROWS), :].astype(BF) for j in range(PAIR_ROWS)])


def padded_latents(new, row):
    lat = new[pl.ds(row, 1), :].astype(F32)
    rows = [lat[:, s * KV : (s + 1) * KV] for s in range(STEPS)]
    return jnp.concatenate(rows + [jnp.zeros((LANES - STEPS, KV), F32)], axis=0).astype(BF)


def by_step(even, odd):
    half = HEADS // 2
    return jnp.concatenate([x[s * half : (s + 1) * half] for s in range(STEPS) for x in (even, odd)], axis=0)


def penalty(length):
    column = lax.broadcasted_iota(jnp.int32, (8, CTX + LANES), 1)
    position = jnp.where(column < PAIRS, 2 * column, 2 * (column - PAIRS) + 1)
    step = lax.broadcasted_iota(jnp.int32, (8, CTX + LANES), 0)
    live = jnp.where(column < CTX, position, column - CTX) < jnp.where(column < CTX, length, step + 1)
    return jnp.where(live, 0.0, -jnp.inf).astype(F32)


def probabilities(queries, keys, penalties):
    scores = lax.dot_general(queries, keys, (((1,), (1,)), ((), ())), preferred_element_type=F32) * score_scale
    rows = [scores[s * HEADS : (s + 1) * HEADS] + penalties[s : s + 1] for s in range(STEPS)]
    scores = jnp.concatenate(rows, axis=0)
    exps = jnp.exp(scores - jnp.max(scores, axis=1, keepdims=True))
    return (exps * (1.0 / jnp.sum(exps, axis=1, keepdims=True))).astype(BF)


def put_context(rows, token, step, context):
    tokens = rows.shape[0] // CHUNKS
    half, chunks = HEADS // 2, LAT // LANES
    for parity in range(2):
        for k in range(chunks):
            at = (step * HEADS * chunks + parity * chunks + k) * tokens + token % tokens
            rows[pl.ds(at, half, 2 * chunks * tokens), :] = context[
                parity * half : (parity + 1) * half, k * LANES : (k + 1) * LANES
            ]


def cut_tiles(flat, out):
    for g in range(PAIRS // 16):
        for j in range(PAIR_ROWS):
            tile = flat[pl.ds(g * 16 * PAIR_ROWS + j, 16, PAIR_ROWS), :]
            out[pl.ds((g * PAIR_ROWS + j) * 16, 16), :] = tile.astype(BF)


def fresh_kernel(src, out, flat):
    flat_row(src, 0, flat, CACHE_ROWS)
    pool = lax.axis_index("pool")

    @pl.when(pool == 0)
    def _():
        cut_tiles(flat, out)

    @pl.when(pool == 1)
    def _():
        out[...] = flat[...].astype(BF)


def fresh_rows(fresh):
    return pl.pallas_call(
        fresh_kernel,
        out_shape=jax.ShapeDtypeStruct((CACHE_ROWS, LANES), BF),
        in_specs=[in_vmem],
        out_specs=in_vmem,
        scratch_shapes=[pltpu.VMEM((CACHE_ROWS, LANES), F32)],
        compiler_params=small,
        name="fresh_rows",
    )(fresh)


def taken_kernel(rows, out, plain, flat, cut, sems):
    @pl.when(lax.axis_index("pool") == 0)
    def _():
        load = pltpu.make_async_copy(rows, plain, sems.at[0])
        load.start()
        load.wait()
        flat[...] = plain[...].astype(F32)
        cut_tiles(flat, cut)
        store = pltpu.make_async_copy(cut, out, sems.at[1])
        store.start()
        store.wait()


def taken_tiles(rows):
    return pl.pallas_call(
        taken_kernel,
        out_shape=jax.ShapeDtypeStruct(rows.shape, BF),
        in_specs=[pl.BlockSpec(memory_space=pl.ANY)],
        out_specs=pl.BlockSpec(memory_space=pl.ANY),
        scratch_shapes=[
            pltpu.VMEM((CACHE_ROWS, LANES), BF),
            pltpu.VMEM((CACHE_ROWS, LANES), F32),
            pltpu.VMEM((CACHE_ROWS, LANES), BF),
            pltpu.SemaphoreType.DMA((2,)),
        ],
        input_output_aliases={0: 0},
        compiler_params=small,
        name="taken_tiles",
    )(rows)


def gather_kernel(sources, blocks, out):
    last = out.shape[0] - 1
    for d in range(last + 1):
        out[d] = blocks[last - sources[last - d]]


def gather_blocks(sources, blocks):
    return pl.pallas_call(
        gather_kernel,
        out_shape=jax.ShapeDtypeStruct(blocks.shape, BF),
        in_specs=[in_smem, in_vmem],
        out_specs=in_vmem,
        compiler_params=small,
        name="gather_blocks",
    )(sources, blocks)


def pair_rows(both, rows, place):
    for c in range(place.start, place.start + place.size, LANES):
        rows[pl.ds(c, LANES)] = both[pl.ds(2 * c, 2 * LANES), :].astype(BF).reshape(LANES, 2, LANES)


def resident_kernel(
    lengths,
    fresh_lengths,
    matching,
    queries,
    new,
    caches,
    out,
    third,
    last_queries,
    last_latents,
    last_penalty,
    query_flat,
    cache_flat,
    both,
    rows,
    sem,
):
    def queries_of(row):
        flat_row(queries, row, query_flat, QUERY_ROWS)
        return by_step(*strided_halves(query_flat, QUERY_ROWS // PAIR_ROWS))

    for r in range(ROWS - 1):
        flat_row(caches, r, cache_flat, CACHE_ROWS)
        keys = jnp.concatenate([*strided_halves(cache_flat, PAIRS), padded_latents(new, r)], axis=0)
        probs = probabilities(queries_of(r), keys, penalty(lengths[r]))
        context = jnp.dot(probs, keys[:, :LAT], preferred_element_type=F32)
        for step in range(STEPS):
            put_context(both if r < 2 else third, r, step, context[step * HEADS : (step + 1) * HEADS])
        if r == 1:
            pair_rows(both, rows, pl.ds(0, CHUNKS))
            copy = pltpu.make_async_copy(rows, out.at[:, 0], sem)
            copy.start()
    last_queries[...] = queries_of(ROWS - 1)
    last_latents[...] = padded_latents(new, ROWS - 1)
    pool = lax.axis_index("pool")
    last_penalty[...] = penalty(fresh_lengths[1 - pool, matching[pool, lax.axis_index("ep")]])
    copy.wait()


def resident_attention(lengths, fresh_lengths, matching, queries, new, caches):
    return pl.pallas_call(
        resident_kernel,
        out_shape=(
            jax.ShapeDtypeStruct((CHUNKS, 2, 2, LANES), BF),
            jax.ShapeDtypeStruct((CHUNKS, LANES), F32),
            jax.ShapeDtypeStruct((STEPS * HEADS, KV), BF),
            jax.ShapeDtypeStruct((LANES, KV), BF),
            jax.ShapeDtypeStruct((8, CTX + LANES), F32),
        ),
        in_specs=[in_smem] * 3 + [in_vmem] * 3,
        out_specs=(pl.BlockSpec(memory_space=pl.ANY),) + (in_vmem,) * 4,
        scratch_shapes=[
            pltpu.VMEM((QUERY_ROWS, LANES), F32),
            pltpu.VMEM((CACHE_ROWS, LANES), F32),
            pltpu.VMEM((2 * CHUNKS, LANES), F32),
            pltpu.VMEM((CHUNKS, 2, LANES), BF),
            pltpu.SemaphoreType.DMA(()),
        ],
        compiler_params=pltpu.CompilerParams(vmem_limit_bytes=32 << 20),
        cost_estimate=pl.CostEstimate(flops=10**9, bytes_accessed=8 << 20, transcendentals=400000),
        name="resident_attention",
    )(lengths, fresh_lengths, matching, queries, new, caches)


def arrived_kernel(penalties, queries, latents, tiles, third, before, out, both, rows, sems):
    parts = tiles[...].reshape(PAIRS // 16, PAIR_ROWS, 16, LANES)
    halved = halves([parts[:, j].reshape(PAIRS, LANES) for j in range(PAIR_ROWS)])
    keys = jnp.concatenate([*halved, latents[...]], axis=0)
    both[pl.ds(0, CHUNKS, 2), :] = third[...]
    probs = probabilities(queries[...], keys, penalties[...])
    values = keys[:, :LAT]
    copies = []
    size = CHUNKS // STEPS
    for step in range(STEPS):
        context = jnp.dot(probs[step * HEADS : (step + 1) * HEADS], values, preferred_element_type=F32)
        put_context(both, ROWS - 1, step, context)
        place = pl.ds(step * size, size)
        pair_rows(both, rows, place)
        copy = pltpu.make_async_copy(rows.at[place], out.at[place, 1], sems.at[step])
        copy.start()
        copies.append(copy)
    for copy in copies:
        copy.wait()


def arrived_attention(penalties, queries, latents, tiles, third, before):
    whole = pl.BlockSpec(memory_space=pl.ANY)
    return pl.pallas_call(
        arrived_kernel,
        out_shape=jax.ShapeDtypeStruct(before.shape, BF),
        in_specs=[in_vmem] * 5 + [whole],
        out_specs=whole,
        scratch_shapes=[
            pltpu.VMEM((2 * CHUNKS, LANES), F32),
            pltpu.VMEM((CHUNKS, 2, LANES), BF),
            pltpu.SemaphoreType.DMA((STEPS,)),
        ],
        input_output_aliases={5: 0},
        compiler_params=pltpu.CompilerParams(vmem_limit_bytes=24 << 20),
        name="arrived_attention",
    )(penalties, queries, latents, tiles, third, before)


def exchange(blocks):
    places = list(range(blocks.shape[0]))[::-1]
    return lax.all_to_all(blocks, "ep", split_axis=0, concat_axis=0, tiled=True, axis_index_groups=[places])


def per_device(queries, new_latent, resident_cache, resident_len, fresh_cache, fresh_len, matching):
    group_count = lax.axis_size("ep")
    pool_index = lax.axis_index("pool")
    own_sources = matching[pool_index]
    tiles = taken_tiles(lax.ppermute(fresh_rows(fresh_cache), "pool", [(0, 1), (1, 0)]))
    blocks = tiles.reshape(group_count, PAIR_ROWS, 2, LANES)
    blocks = exchange(blocks)
    out, third, last_queries, last_latents, penalties = resident_attention(
        resident_len, fresh_len, matching, queries, new_latent, resident_cache
    )
    blocks, third = lax.optimization_barrier((blocks, third))
    blocks = gather_blocks(own_sources, blocks)
    blocks = exchange(blocks)
    tiles = blocks.reshape(CACHE_ROWS, LANES)
    out = arrived_attention(penalties, last_queries, last_latents, tiles, third, out)
    return out.transpose(1, 2, 0, 3).reshape(ROWS, -1)


def solution(mesh):
    return jax.shard_map(
        per_device,
        mesh=mesh,
        in_specs=(
            P(("pool", "ep"), None),
            P(("pool", "ep"), None),
            P(("pool", "ep"), None),
            P(("pool", "ep")),
            P(("pool", "ep"), None),
            P(),
            P(),
        ),
        out_specs=P(("pool", "ep"), None),
        check_vma=False,
    )
```

```python
import jax
import jax.numpy as jnp
from jax import lax
from jax.experimental import pallas as pl
from jax.experimental.pallas import tpu as pltpu
from jax.sharding import PartitionSpec as P

LAT = 512
KV = 576
STEPS = 2
HEADS = 128
CTX = 512
ROWS = 4
LANES = 128
PAIRS = CTX // 2
PAIR_ROWS = 2 * KV // LANES
CACHE_ROWS = CTX * KV // LANES
QUERY_ROWS = STEPS * HEADS * KV // LANES
CHUNKS = STEPS * HEADS * LAT // LANES
BF, F32 = jnp.bfloat16, jnp.float32

score_scale = 192.0 ** (-0.5)
in_vmem = pl.BlockSpec(memory_space=pltpu.VMEM)
in_smem = pl.BlockSpec(memory_space=pltpu.SMEM)
small = pltpu.CompilerParams(vmem_limit_bytes=8 << 20)


def flat_row(src, row, flat, count):
    for at in range(0, count, LANES):
        piece = src[pl.ds(row, 1), pl.ds(at * LANES, LANES * LANES)]
        flat[pl.ds(at, LANES), :] = piece.astype(F32).reshape(LANES, LANES)


def halves(tiles):
    even = jnp.concatenate(tiles[:5], axis=1)[:, :KV]
    odd = jnp.concatenate(tiles[4:], axis=1)[:, KV - LAT : KV - LAT + KV]
    return even, odd


def strided_halves(flat, pairs):
    return halves([flat[pl.ds(j, pairs, PAIR_ROWS), :].astype(BF) for j in range(PAIR_ROWS)])


def padded_latents(new, row):
    lat = new[pl.ds(row, 1), :].astype(F32)
    rows = [lat[:, s * KV : (s + 1) * KV] for s in range(STEPS)]
    return jnp.concatenate(rows + [jnp.zeros((LANES - STEPS, KV), F32)], axis=0).astype(BF)


def by_step(even, odd):
    half = HEADS // 2
    return jnp.concatenate([x[s * half : (s + 1) * half] for s in range(STEPS) for x in (even, odd)], axis=0)


def penalty(length):
    column = lax.broadcasted_iota(jnp.int32, (8, CTX + LANES), 1)
    position = jnp.where(column < PAIRS, 2 * column, 2 * (column - PAIRS) + 1)
    step = lax.broadcasted_iota(jnp.int32, (8, CTX + LANES), 0)
    live = jnp.where(column < CTX, position, column - CTX) < jnp.where(column < CTX, length, step + 1)
    return jnp.where(live, 0.0, -jnp.inf).astype(F32)


def probabilities(queries, keys, penalties):
    scores = lax.dot_general(queries, keys, (((1,), (1,)), ((), ())), preferred_element_type=F32) * score_scale
    rows = [scores[s * HEADS : (s + 1) * HEADS] + penalties[s : s + 1] for s in range(STEPS)]
    scores = jnp.concatenate(rows, axis=0)
    exps = jnp.exp(scores - jnp.max(scores, axis=1, keepdims=True))
    return (exps * (1.0 / jnp.sum(exps, axis=1, keepdims=True))).astype(BF)


def put_context(rows, token, step, context):
    tokens = rows.shape[0] // CHUNKS
    half, chunks = HEADS // 2, LAT // LANES
    for parity in range(2):
        for k in range(chunks):
            at = (step * HEADS * chunks + parity * chunks + k) * tokens + token % tokens
            rows[pl.ds(at, half, 2 * chunks * tokens), :] = context[
                parity * half : (parity + 1) * half, k * LANES : (k + 1) * LANES
            ]


def cut_tiles(flat, out):
    for g in range(PAIRS // 16):
        for j in range(PAIR_ROWS):
            tile = flat[pl.ds(g * 16 * PAIR_ROWS + j, 16, PAIR_ROWS), :]
            out[pl.ds((g * PAIR_ROWS + j) * 16, 16), :] = tile.astype(BF)


def fresh_kernel(src, out, flat):
    flat_row(src, 0, flat, CACHE_ROWS)
    pool = lax.axis_index("pool")

    @pl.when(pool == 0)
    def _():
        cut_tiles(flat, out)

    @pl.when(pool == 1)
    def _():
        out[...] = flat[...].astype(BF)


def fresh_rows(fresh):
    return pl.pallas_call(
        fresh_kernel,
        out_shape=jax.ShapeDtypeStruct((CACHE_ROWS, LANES), BF),
        in_specs=[in_vmem],
        out_specs=in_vmem,
        scratch_shapes=[pltpu.VMEM((CACHE_ROWS, LANES), F32)],
        compiler_params=small,
        name="fresh_rows",
    )(fresh)


def taken_kernel(rows, out, plain, flat, cut, sems):
    @pl.when(lax.axis_index("pool") == 0)
    def _():
        load = pltpu.make_async_copy(rows, plain, sems.at[0])
        load.start()
        load.wait()
        flat[...] = plain[...].astype(F32)
        cut_tiles(flat, cut)
        store = pltpu.make_async_copy(cut, out, sems.at[1])
        store.start()
        store.wait()


def taken_tiles(rows):
    return pl.pallas_call(
        taken_kernel,
        out_shape=jax.ShapeDtypeStruct(rows.shape, BF),
        in_specs=[pl.BlockSpec(memory_space=pl.ANY)],
        out_specs=pl.BlockSpec(memory_space=pl.ANY),
        scratch_shapes=[
            pltpu.VMEM((CACHE_ROWS, LANES), BF),
            pltpu.VMEM((CACHE_ROWS, LANES), F32),
            pltpu.VMEM((CACHE_ROWS, LANES), BF),
            pltpu.SemaphoreType.DMA((2,)),
        ],
        input_output_aliases={0: 0},
        compiler_params=small,
        name="taken_tiles",
    )(rows)


def gather_kernel(sources, blocks, out):
    last = out.shape[0] - 1
    for d in range(last + 1):
        out[d] = blocks[last - sources[last - d]]


def gather_blocks(sources, blocks):
    return pl.pallas_call(
        gather_kernel,
        out_shape=jax.ShapeDtypeStruct(blocks.shape, BF),
        in_specs=[in_smem, in_vmem],
        out_specs=in_vmem,
        compiler_params=small,
        name="gather_blocks",
    )(sources, blocks)


def pair_rows(both, rows, place):
    for c in range(place.start, place.start + place.size, LANES):
        rows[pl.ds(c, LANES)] = both[pl.ds(2 * c, 2 * LANES), :].astype(BF).reshape(LANES, 2, LANES)


def resident_kernel(
    lengths,
    fresh_lengths,
    matching,
    queries,
    new,
    caches,
    out,
    third,
    last_queries,
    last_latents,
    last_penalty,
    query_flat,
    cache_flat,
    both,
    rows,
    sem,
):
    def queries_of(row):
        flat_row(queries, row, query_flat, QUERY_ROWS)
        return by_step(*strided_halves(query_flat, QUERY_ROWS // PAIR_ROWS))

    for r in range(ROWS - 1):
        flat_row(caches, r, cache_flat, CACHE_ROWS)
        keys = jnp.concatenate([*strided_halves(cache_flat, PAIRS), padded_latents(new, r)], axis=0)
        probs = probabilities(queries_of(r), keys, penalty(lengths[r]))
        context = jnp.dot(probs, keys[:, :LAT], preferred_element_type=F32)
        for step in range(STEPS):
            put_context(both if r < 2 else third, r, step, context[step * HEADS : (step + 1) * HEADS])
        if r == 1:
            pair_rows(both, rows, pl.ds(0, CHUNKS))
            copy = pltpu.make_async_copy(rows, out.at[:, 0], sem)
            copy.start()
    last_queries[...] = queries_of(ROWS - 1)
    last_latents[...] = padded_latents(new, ROWS - 1)
    pool = lax.axis_index("pool")
    last_penalty[...] = penalty(fresh_lengths[1 - pool, matching[pool, lax.axis_index("ep")]])
    copy.wait()


def resident_attention(lengths, fresh_lengths, matching, queries, new, caches):
    return pl.pallas_call(
        resident_kernel,
        out_shape=(
            jax.ShapeDtypeStruct((CHUNKS, 2, 2, LANES), BF),
            jax.ShapeDtypeStruct((CHUNKS, LANES), F32),
            jax.ShapeDtypeStruct((STEPS * HEADS, KV), BF),
            jax.ShapeDtypeStruct((LANES, KV), BF),
            jax.ShapeDtypeStruct((8, CTX + LANES), F32),
        ),
        in_specs=[in_smem] * 3 + [in_vmem] * 3,
        out_specs=(pl.BlockSpec(memory_space=pl.ANY),) + (in_vmem,) * 4,
        scratch_shapes=[
            pltpu.VMEM((QUERY_ROWS, LANES), F32),
            pltpu.VMEM((CACHE_ROWS, LANES), F32),
            pltpu.VMEM((2 * CHUNKS, LANES), F32),
            pltpu.VMEM((CHUNKS, 2, LANES), BF),
            pltpu.SemaphoreType.DMA(()),
        ],
        compiler_params=pltpu.CompilerParams(vmem_limit_bytes=32 << 20),
        cost_estimate=pl.CostEstimate(flops=10**9, bytes_accessed=8 << 20, transcendentals=400000),
        name="resident_attention",
    )(lengths, fresh_lengths, matching, queries, new, caches)


def arrived_kernel(penalties, queries, latents, tiles, third, before, out, both, rows, sems):
    parts = tiles[...].reshape(PAIRS // 16, PAIR_ROWS, 16, LANES)
    halved = halves([parts[:, j].reshape(PAIRS, LANES) for j in range(PAIR_ROWS)])
    keys = jnp.concatenate([*halved, latents[...]], axis=0)
    both[pl.ds(0, CHUNKS, 2), :] = third[...]
    probs = probabilities(queries[...], keys, penalties[...])
    values = keys[:, :LAT]
    copies = []
    size = CHUNKS // STEPS
    for step in range(STEPS):
        context = jnp.dot(probs[step * HEADS : (step + 1) * HEADS], values, preferred_element_type=F32)
        put_context(both, ROWS - 1, step, context)
        place = pl.ds(step * size, size)
        pair_rows(both, rows, place)
        copy = pltpu.make_async_copy(rows.at[place], out.at[place, 1], sems.at[step])
        copy.start(priority=step)
        copies.append(copy)
    for copy in copies:
        copy.wait()


def arrived_attention(penalties, queries, latents, tiles, third, before):
    whole = pl.BlockSpec(memory_space=pl.ANY)
    return pl.pallas_call(
        arrived_kernel,
        out_shape=jax.ShapeDtypeStruct(before.shape, BF),
        in_specs=[in_vmem] * 5 + [whole],
        out_specs=whole,
        scratch_shapes=[
            pltpu.VMEM((2 * CHUNKS, LANES), F32),
            pltpu.VMEM((CHUNKS, 2, LANES), BF),
            pltpu.SemaphoreType.DMA((STEPS,)),
        ],
        input_output_aliases={5: 0},
        compiler_params=pltpu.CompilerParams(vmem_limit_bytes=24 << 20),
        name="arrived_attention",
    )(penalties, queries, latents, tiles, third, before)


def exchange(blocks):
    places = list(range(blocks.shape[0]))[::-1]
    return lax.all_to_all(blocks, "ep", split_axis=0, concat_axis=0, tiled=True, axis_index_groups=[places])


def per_device(queries, new_latent, resident_cache, resident_len, fresh_cache, fresh_len, matching):
    group_count = lax.axis_size("ep")
    pool_index = lax.axis_index("pool")
    own_sources = matching[pool_index]
    tiles = taken_tiles(lax.ppermute(fresh_rows(fresh_cache), "pool", [(0, 1), (1, 0)]))
    blocks = tiles.reshape(group_count, PAIR_ROWS, 2, LANES)
    blocks = exchange(blocks)
    out, third, last_queries, last_latents, penalties = resident_attention(
        resident_len, fresh_len, matching, queries, new_latent, resident_cache
    )
    blocks, third = lax.optimization_barrier((blocks, third))
    blocks = gather_blocks(own_sources, blocks)
    blocks = exchange(blocks)
    tiles = blocks.reshape(CACHE_ROWS, LANES)
    out = arrived_attention(penalties, last_queries, last_latents, tiles, third, out)
    return out.transpose(1, 2, 0, 3).reshape(ROWS, -1)


def solution(mesh):
    return jax.shard_map(
        per_device,
        mesh=mesh,
        in_specs=(
            P(("pool", "ep"), None),
            P(("pool", "ep"), None),
            P(("pool", "ep"), None),
            P(("pool", "ep")),
            P(("pool", "ep"), None),
            P(),
            P(),
        ),
        out_specs=P(("pool", "ep"), None),
        check_vma=False,
    )
```
